32 devices in a mesh: row: 2 (over y), col: 16 (over z, x, core).
Axes of the slice: x: 2, y: 2, z: 4, core: 2. Of those that a mesh axis runs over, the one named last changes fastest.
Arguments:
- pair_density: bfloat16 [2048, 4000], P(('row', 'col')), may hold values from -1 to 1
- coulomb: float32 [4000], replicated, may hold values from 0.1 to 10
Outputs:
- kernel: float32 [2048, 16, 128], P('row', 'col')
The draws below stay inside these ranges and needn't reach their ends.
All inputs are finite; a program needn't handle non-finite values.
Results may differ from the reference program's by a relative error of at most 0.0038.
Values may be sent and summed in bfloat16 or wider, within the bound.
A program may use at most 128 MiB of HBM per device.

```python
import math
import jax
import jax.numpy as jnp

NG = 4000
NB = 64
NT = 2048
N_ROW = 2
N_COL = 16


def levels(key, dims, cuts, low, largest):
    def one(position, blocks):
        draws = jax.random.uniform(jax.random.fold_in(jax.random.fold_in(key, 6), position), (blocks,), jnp.float32, low / len(cuts), largest / len(cuts))
        return jnp.repeat(jnp.exp(draws), dims[position] // blocks).reshape((-1,) + (1,) * (len(dims) - position - 1))

    factor_of = one(*cuts[0])
    for cut in cuts[1:]:
        factor_of = factor_of * one(*cut)
    return factor_of


def centred(stream_key, extent, scale, bound, shards=(), held_as=jnp.bfloat16):
    entries = scale * jax.random.normal(stream_key, extent, jnp.float32)
    if shards:
        entries = entries * levels(stream_key, extent, shards, -0.22, 0.18)
    return jnp.clip(entries, -bound, bound).astype(held_as)


def setup_inputs(seed: int = 0) -> dict:
    arg_keys = jax.random.split(jax.random.key(seed), 3)
    return {
        "pair_density": centred(arg_keys[0], (NT, NG), (0.55 * NG ** -0.25), 1.0, ((0, 32),)),
        "coulomb": jnp.clip(jnp.exp(jax.random.uniform(arg_keys[1], (NG,), jnp.float32, math.log(0.1), math.log(10.0))), 0.1, 10.0),
    }


def reference(pair_density, coulomb):
    scaled = (jnp.sqrt(coulomb)[None, :] * pair_density.astype(jnp.float32)).astype(jnp.bfloat16)
    full = jnp.dot(scaled, scaled.T, preferred_element_type=jnp.float32)
    arranged = full.reshape(NT, N_ROW, N_COL, NB).transpose(0, 2, 1, 3)
    return arranged.reshape(NT, N_COL, N_ROW * NB)
```

```python
import functools

import jax
import jax.numpy as jnp
from jax import lax
from jax.experimental import pallas as pl
from jax.experimental.pallas import tpu as pltpu
from jax.sharding import PartitionSpec as P

UP, DOWN, SIDE, TWIN = range(4)
PARTS = 4


def body(rows, cols, pair_ref, root_ref, out_ref, held, piece, send_sem, recv_sem, row_send, row_recv):
    band = pair_ref.shape[0]
    part = band // PARTS
    line = cols // 4
    my_row = lax.axis_index("row")
    me = lax.axis_index("col")
    core = lax.rem(me, 2)
    x = lax.rem(me // 2, 2)
    z = me // 4

    def col_of(zz, xx, cc):
        return (zz * 2 + xx) * 2 + cc

    def device(way):
        if way == UP:
            target = col_of(z + 1, x, core)
        elif way == DOWN:
            target = col_of(z - 1, x, core)
        elif way == SIDE:
            target = col_of(z, 1 - x, core)
        else:
            target = col_of(z, x, 1 - core)
        return (my_row, target)

    def window(slot, k):
        return pl.ds(pl.multiple_of(slot * band + k * part, part), part)

    def copy(way, slot, k):
        return pltpu.make_async_remote_copy(
            src_ref=held.at[window(slot, k)],
            dst_ref=held.at[window(slot, k)],
            send_sem=send_sem.at[way, slot, k],
            recv_sem=recv_sem.at[slot, k],
            device_id=device(way),
            device_id_type=pl.DeviceIdType.MESH,
        )

    def arrive(slot, k):
        copy(SIDE, slot, k).wait_recv()

    def row_copy(step, k):
        target = lax.rem(my_row + step, rows)
        return pltpu.make_async_remote_copy(
            src_ref=held.at[window(me, k)],
            dst_ref=piece.at[window(my_row, k)],
            send_sem=row_send.at[target, k],
            recv_sem=row_recv.at[my_row, k],
            device_id=(target, me),
            device_id_type=pl.DeviceIdType.MESH,
        )

    def row_arrive(step, k):
        source = lax.rem(my_row + step, rows)
        pltpu.make_async_remote_copy(
            src_ref=piece.at[window(source, k)],
            dst_ref=piece.at[window(source, k)],
            send_sem=row_send.at[source, k],
            recv_sem=row_recv.at[source, k],
            device_id=(source, me),
            device_id_type=pl.DeviceIdType.MESH,
        ).wait_recv()

    has_up = z < line - 1
    has_down = z > 0

    barrier = pltpu.get_barrier_semaphore()

    def greet(target):
        pl.semaphore_signal(barrier, inc=1, device_id=target, device_id_type=pl.DeviceIdType.MESH)

    greet(device(SIDE))
    greet(device(TWIN))
    for step in range(1, rows):
        greet((lax.rem(my_row + step, rows), me))

    @pl.when(has_up)
    def _():
        greet(device(UP))

    @pl.when(has_down)
    def _():
        greet(device(DOWN))

    for k in range(PARTS):
        here = pl.ds(k * part, part)
        value = (root_ref[...] * pair_ref[here].astype(jnp.float32)).astype(jnp.bfloat16)
        held[window(me, k)] = value
        piece[window(my_row, k)] = value
        if k == 0:
            ends = (z == 0).astype(jnp.int32) + (z == line - 1).astype(jnp.int32)
            pl.semaphore_wait(barrier, 3 + rows - ends)

        @pl.when(has_up)
        def _():
            copy(UP, me, k).start()

        @pl.when(has_down)
        def _():
            copy(DOWN, me, k).start()

        copy(SIDE, me, k).start()
        copy(TWIN, me, k).start()
        for step in range(1, rows):
            row_copy(step, k).start()

    def forward(d, _):
        def each(k, _):
            @pl.when(z - d >= 0)
            def _():
                slot = col_of(z - d, x, core)
                arrive(slot, k)

                @pl.when(has_up)
                def _():
                    copy(UP, slot, k).start()

                copy(SIDE, slot, k).start()
                copy(TWIN, slot, k).start()

            @pl.when(z + d < line)
            def _():
                slot = col_of(z + d, x, core)
                arrive(slot, k)

                @pl.when(has_down)
                def _():
                    copy(DOWN, slot, k).start()

                copy(SIDE, slot, k).start()
                copy(TWIN, slot, k).start()

            return 0

        return lax.fori_loop(0, PARTS, each, 0)

    lax.fori_loop(1, line, forward, 0)

    def row_wait(k, _):
        for step in range(1, rows):
            row_arrive(step, k)
        return 0

    lax.fori_loop(0, PARTS, row_wait, 0)

    def product(zz, xx):
        def each(k, _):
            arrive(col_of(zz, xx, 1 - core), k)
            return 0

        lax.fori_loop(0, PARTS, each, 0)
        start = pl.multiple_of(col_of(zz, xx, 0) * band, 2 * band)
        out_ref[pl.ds(start, 2 * band)] = lax.dot_general(
            held[pl.ds(start, 2 * band)],
            piece[...],
            (((1,), (1,)), ((), ())),
            preferred_element_type=jnp.float32,
        )

    def settle(d, _):
        def one(zz):
            def each(k, _):
                slot = col_of(zz, 1 - x, core)
                arrive(slot, k)
                copy(TWIN, slot, k).start()
                return 0

            product(zz, x)
            lax.fori_loop(0, PARTS, each, 0)
            product(zz, 1 - x)

        def both(sign, _):
            zz = z + sign * d

            @pl.when((zz >= 0) & (zz < line) & ((d > 0) | (sign > 0)))
            def _():
                one(zz)

            return 0

        return lax.fori_loop(0, 2, lambda s, c: both(2 * s - 1, c), 0)

    lax.fori_loop(0, line, settle, 0)

    def drain(zz, _):
        def each(k, _):
            mine = col_of(zz, x, core)
            copy(SIDE, mine, k).wait_send()
            copy(TWIN, mine, k).wait_send()
            copy(TWIN, col_of(zz, 1 - x, core), k).wait_send()

            @pl.when(has_up & (zz <= z))
            def _():
                copy(UP, mine, k).wait_send()

            @pl.when(has_down & (zz >= z))
            def _():
                copy(DOWN, mine, k).wait_send()

            return 0

        return lax.fori_loop(0, PARTS, each, 0)

    lax.fori_loop(0, line, drain, 0)

    def row_drain(k, _):
        for step in range(1, rows):
            row_copy(step, k).wait_send()
        return 0

    lax.fori_loop(0, PARTS, row_drain, 0)


def on_device(rows, cols, pair_density, coulomb):
    band, comps = pair_density.shape
    root = jnp.sqrt(coulomb)[None, :]
    vmem = pl.BlockSpec(memory_space=pltpu.VMEM)
    kernel = pl.pallas_call(
        functools.partial(body, rows, cols),
        out_shape=jax.ShapeDtypeStruct((cols * band, rows * band), jnp.float32),
        in_specs=[vmem, vmem],
        out_specs=vmem,
        scratch_shapes=[
            pltpu.VMEM((cols * band, comps), jnp.bfloat16),
            pltpu.VMEM((rows * band, comps), jnp.bfloat16),
            pltpu.SemaphoreType.DMA((4, cols, PARTS)),
            pltpu.SemaphoreType.DMA((cols, PARTS)),
            pltpu.SemaphoreType.DMA((rows, PARTS)),
            pltpu.SemaphoreType.DMA((rows, PARTS)),
        ],
        compiler_params=pltpu.CompilerParams(
            collective_id=0, has_side_effects=True, vmem_limit_bytes=48 * 1024 * 1024
        ),
        cost_estimate=pl.CostEstimate(
            flops=2 * cols * rows * band * band * comps,
            bytes_accessed=2 * band * comps + 4 * cols * rows * band * band,
            transcendentals=0,
        ),
    )(pair_density, root)
    return kernel.reshape(cols * band, 1, rows * band)


def solution(mesh):
    rows, cols = mesh.shape["row"], mesh.shape["col"]
    in_specs = (P(("row", "col"), None), P())
    out_specs = P("row", "col", None)
    return jax.shard_map(
        functools.partial(on_device, rows, cols),
        mesh=mesh,
        in_specs=in_specs,
        out_specs=out_specs,
        check_vma=False,
    )
```

```python
import functools

import jax
import jax.numpy as jnp
from jax import lax
from jax.experimental import pallas as pl
from jax.experimental.pallas import tpu as pltpu
from jax.sharding import PartitionSpec as P

UP, DOWN, SIDE, TWIN = range(4)
PARTS = 4
SWAPPED = 2


def body(rows, cols, pair_ref, weight_ref, out_ref, held, piece, lent, *sems):
    send_sem, recv_sem, row_send, row_recv, lent_send, lent_recv = sems
    band = pair_ref.shape[0]
    part = band // PARTS
    line = cols // 4
    my_row = lax.axis_index("row")
    me = lax.axis_index("col")
    core = lax.rem(me, 2)
    x = lax.rem(me // 2, 2)
    z = me // 4

    def col_of(zz, xx, cc):
        return (zz * 2 + xx) * 2 + cc

    def device(way):
        if way == UP:
            target = col_of(z + 1, x, core)
        elif way == DOWN:
            target = col_of(z - 1, x, core)
        elif way == SIDE:
            target = col_of(z, 1 - x, core)
        else:
            target = col_of(z, x, 1 - core)
        return (my_row, target)

    def window(slot, k):
        return pl.ds(pl.multiple_of(slot * band + k * part, part), part)

    def copy(way, slot, k):
        return pltpu.make_async_remote_copy(
            src_ref=held.at[window(slot, k)],
            dst_ref=held.at[window(slot, k)],
            send_sem=send_sem.at[way, slot, k],
            recv_sem=recv_sem.at[slot, k],
            device_id=device(way),
            device_id_type=pl.DeviceIdType.MESH,
        )

    def arrive(slot, k):
        copy(SIDE, slot, k).wait_recv()

    def row_copy(step, ward, k):
        target = lax.rem(my_row + step, rows)
        return pltpu.make_async_remote_copy(
            src_ref=held.at[window(ward_slot if ward else me, k)],
            dst_ref=piece.at[window(ward * rows + my_row, k)],
            send_sem=row_send.at[ward, target, k],
            recv_sem=row_recv.at[ward, my_row, k],
            device_id=(target, me),
            device_id_type=pl.DeviceIdType.MESH,
        )

    def row_arrive(step, ward, k):
        source = lax.rem(my_row + step, rows)
        pltpu.make_async_remote_copy(
            src_ref=piece.at[window(ward * rows + source, k)],
            dst_ref=piece.at[window(ward * rows + source, k)],
            send_sem=row_send.at[ward, source, k],
            recv_sem=row_recv.at[ward, source, k],
            device_id=(source, me),
            device_id_type=pl.DeviceIdType.MESH,
        ).wait_recv()

    def chip_rows(zz, xx):
        return pl.ds(pl.multiple_of(col_of(zz, xx, 0) * band, 2 * band), 2 * band)

    def lent_copy(zz, xx):
        return pltpu.make_async_remote_copy(
            src_ref=lent.at[chip_rows(zz, xx)],
            dst_ref=lent.at[chip_rows(zz, xx)],
            send_sem=lent_send.at[zz, xx],
            recv_sem=lent_recv.at[zz, xx],
            device_id=(my_row, ward_slot),
            device_id_type=pl.DeviceIdType.MESH,
        )

    end = (z == 0) | (z == line - 1)
    inner = jnp.logical_not(end)
    helper = (z == 1) | (z == line - 2)
    ward_z = jnp.where(z == 1, 0, jnp.where(end, jnp.where(z == 0, 1, line - 2), line - 1))
    ward_slot = col_of(ward_z, x, core)
    to_up = z < line - 2
    to_down = z > 1

    def goes_side(zz, k):
        far = (zz < z - 1) | (zz > z + 1)
        middle = (zz > 0) & (zz < line - 1) & (k >= SWAPPED)
        return (zz == z) | (inner & (far | middle))

    has_up = z < line - 1
    has_down = z > 0

    barrier = pltpu.get_barrier_semaphore()

    def greet(target):
        pl.semaphore_signal(barrier, inc=1, device_id=target, device_id_type=pl.DeviceIdType.MESH)

    greet(device(SIDE))
    greet(device(TWIN))
    for step in range(1, rows):
        greet((lax.rem(my_row + step, rows), me))

    @pl.when(has_up)
    def _():
        greet(device(UP))

    @pl.when(has_down)
    def _():
        greet(device(DOWN))

    root = jnp.sqrt(weight_ref[...])
    for k in range(PARTS):
        here = pl.ds(k * part, part)
        value = (root * pair_ref[here].astype(jnp.float32)).astype(jnp.bfloat16)
        held[window(me, k)] = value

        @pl.when(inner)
        def _():
            piece[window(my_row, k)] = value

        if k == 0:
            ends = (z == 0).astype(jnp.int32) + (z == line - 1).astype(jnp.int32)
            pl.semaphore_wait(barrier, 3 + rows - ends)

        @pl.when(to_up)
        def _():
            copy(UP, me, k).start()

        @pl.when(to_down)
        def _():
            copy(DOWN, me, k).start()

        copy(SIDE, me, k).start()

        @pl.when(inner)
        def _():
            copy(TWIN, me, k).start()
            for step in range(1, rows):
                row_copy(step, 0, k).start()

    def relay(zz, way, onward):
        def each(k, _):
            slot = col_of(zz, x, core)
            arrive(slot, k)

            @pl.when(onward)
            def _():
                copy(way, slot, k).start()

            @pl.when(goes_side(zz, k))
            def _():
                copy(SIDE, slot, k).start()

            copy(TWIN, slot, k).start()

            @pl.when(helper & (slot == ward_slot))
            def _():
                piece[window(rows + my_row, k)] = held[window(slot, k)]
                for step in range(1, rows):
                    row_copy(step, 1, k).start()

            return 0

        lax.fori_loop(0, PARTS, each, 0)

    def forward(d, _):
        @pl.when(inner & (z - d >= 0))
        def _():
            relay(z - d, UP, to_up)

        @pl.when(inner & (z + d < line))
        def _():
            relay(z + d, DOWN, to_down)

        return 0

    lax.fori_loop(1, line, forward, 0)

    beside = col_of(z, 1 - x, core)

    def beside_each(k, _):
        arrive(beside, k)

        @pl.when(to_up & (end | (k < SWAPPED)))
        def _():
            copy(UP, beside, k).start()

        @pl.when(to_down & (end | (k < SWAPPED)))
        def _():
            copy(DOWN, beside, k).start()

        @pl.when(inner)
        def _():
            copy(TWIN, beside, k).start()

        return 0

    lax.fori_loop(0, PARTS, beside_each, 0)

    def row_wait(ward):
        def each(k, _):
            for step in range(1, rows):
                row_arrive(step, ward, k)
            return 0

        lax.fori_loop(0, PARTS, each, 0)

    @pl.when(inner)
    def _():
        row_wait(0)

    @pl.when(helper)
    def _():
        row_wait(1)

    def multiply(start, wide):
        return lax.dot_general(
            held[start], piece[: wide * band], (((1,), (1,)), ((), ())), preferred_element_type=jnp.float32
        )

    def product(zz, xx):
        def each(k, _):
            arrive(col_of(zz, xx, 1 - core), k)
            return 0

        lax.fori_loop(0, PARTS, each, 0)
        start = chip_rows(zz, xx)

        @pl.when(helper)
        def _():
            both = multiply(start, 2 * rows)
            lent[start] = both[:, rows * band :]
            lent_copy(zz, xx).start()
            out_ref[start] = both[:, : rows * band]

        if line > 4:

            @pl.when(jnp.logical_not(helper))
            def _():
                out_ref[start] = multiply(start, rows)

    def settle(t, _):
        d = t // 2
        zz = jnp.where(lax.rem(t, 2) == 0, z - d, z + d)

        @pl.when((zz >= 0) & (zz < line) & (t != 0))
        def _():
            def each(k, _):
                slot = col_of(zz, 1 - x, core)
                arrive(slot, k)
                copy(TWIN, slot, k).start()
                return 0

            product(zz, x)

            @pl.when(d > 0)
            def _():
                lax.fori_loop(0, PARTS, each, 0)

            product(zz, 1 - x)

        return 0

    @pl.when(inner)
    def _():
        lax.fori_loop(1, 2 * line, settle, 0)

    @pl.when(end)
    def _():
        def take(t, _):
            d = t // 2
            zz = jnp.where(z == 0, lax.rem(d + 1, line), lax.rem(2 * line - 2 - d, line))
            xx = lax.rem(x + t, 2)
            lent_copy(zz, xx).wait_recv()
            out_ref[chip_rows(zz, xx)] = lent[chip_rows(zz, xx)]
            return 0

        lax.fori_loop(0, 2 * line, take, 0)

    def drain(zz, _):
        def each(k, _):
            mine = col_of(zz, x, core)

            @pl.when(goes_side(zz, k))
            def _():
                copy(SIDE, mine, k).wait_send()

            @pl.when(inner)
            def _():
                copy(TWIN, mine, k).wait_send()
                copy(TWIN, col_of(zz, 1 - x, core), k).wait_send()

            @pl.when(to_up & (zz <= z))
            def _():
                copy(UP, mine, k).wait_send()

            @pl.when(to_down & (zz >= z))
            def _():
                copy(DOWN, mine, k).wait_send()

            return 0

        lax.fori_loop(0, PARTS, each, 0)

        @pl.when(helper)
        def _():
            for xx in range(2):
                lent_copy(zz, xx).wait_send()

        return 0

    lax.fori_loop(0, line, drain, 0)

    def last(k, _):
        @pl.when(to_up & (end | (k < SWAPPED)))
        def _():
            copy(UP, beside, k).wait_send()

        @pl.when(to_down & (end | (k < SWAPPED)))
        def _():
            copy(DOWN, beside, k).wait_send()

        for step in range(1, rows):

            @pl.when(inner)
            def _():
                row_copy(step, 0, k).wait_send()

            @pl.when(helper)
            def _():
                row_copy(step, 1, k).wait_send()

        return 0

    lax.fori_loop(0, PARTS, last, 0)


def on_device(rows, cols, pair_density, coulomb):
    band, comps = pair_density.shape
    weight = coulomb[None, :]
    vmem = pl.BlockSpec(memory_space=pltpu.VMEM)
    kernel = pl.pallas_call(
        functools.partial(body, rows, cols),
        out_shape=jax.ShapeDtypeStruct((cols * band, rows * band), jnp.float32),
        in_specs=[vmem, vmem],
        out_specs=vmem,
        scratch_shapes=[
            pltpu.VMEM((cols * band, comps), jnp.bfloat16),
            pltpu.VMEM((2 * rows * band, comps), jnp.bfloat16),
            pltpu.VMEM((cols * band, rows * band), jnp.float32),
            pltpu.SemaphoreType.DMA((4, cols, PARTS)),
            pltpu.SemaphoreType.DMA((cols, PARTS)),
            pltpu.SemaphoreType.DMA((2, rows, PARTS)),
            pltpu.SemaphoreType.DMA((2, rows, PARTS)),
            pltpu.SemaphoreType.DMA((cols // 4, 2)),
            pltpu.SemaphoreType.DMA((cols // 4, 2)),
        ],
        compiler_params=pltpu.CompilerParams(
            collective_id=0, has_side_effects=True, vmem_limit_bytes=48 * 1024 * 1024
        ),
        cost_estimate=pl.CostEstimate(
            flops=2 * cols * rows * band * band * comps,
            bytes_accessed=2 * band * comps + 4 * cols * rows * band * band,
            transcendentals=0,
        ),
    )(pair_density, weight)
    return kernel.reshape(cols * band, 1, rows * band)


def solution(mesh):
    rows, cols = mesh.shape["row"], mesh.shape["col"]
    in_specs = (P(("row", "col"), None), P())
    out_specs = P("row", "col", None)
    return jax.shard_map(
        functools.partial(on_device, rows, cols),
        mesh=mesh,
        in_specs=in_specs,
        out_specs=out_specs,
        check_vma=False,
    )
```

```python
import functools

import jax
import jax.numpy as jnp
from jax import lax
from jax.experimental import pallas as pl
from jax.experimental.pallas import tpu as pltpu
from jax.sharding import PartitionSpec as P

UP, DOWN, SIDE, TWIN = range(4)
PARTS = 4
SWAPPED = 2
LAG = 2


def body(rows, cols, pair_ref, weight_ref, out_ref, held, piece, lent, *sems):
    send_sem, recv_sem, row_send, row_recv, lent_send, lent_recv = sems
    band = pair_ref.shape[0]
    part = band // PARTS
    line = cols // 4
    my_row = lax.axis_index("row")
    me = lax.axis_index("col")
    core = lax.rem(me, 2)
    x = lax.rem(me // 2, 2)
    z = me // 4

    def col_of(zz, xx, cc):
        return (zz * 2 + xx) * 2 + cc

    def device(way):
        if way == UP:
            target = col_of(z + 1, x, core)
        elif way == DOWN:
            target = col_of(z - 1, x, core)
        elif way == SIDE:
            target = col_of(z, 1 - x, core)
        else:
            target = col_of(z, x, 1 - core)
        return (my_row, target)

    def window(slot, k):
        return pl.ds(pl.multiple_of(slot * band + k * part, part), part)

    def copy(way, slot, k):
        return pltpu.make_async_remote_copy(
            src_ref=held.at[window(slot, k)],
            dst_ref=held.at[window(slot, k)],
            send_sem=send_sem.at[way, slot, k],
            recv_sem=recv_sem.at[slot, k],
            device_id=device(way),
            device_id_type=pl.DeviceIdType.MESH,
        )

    def arrive(slot, k):
        copy(SIDE, slot, k).wait_recv()

    def row_copy(step, ward, k):
        target = lax.rem(my_row + step, rows)
        return pltpu.make_async_remote_copy(
            src_ref=held.at[window(ward_slot if ward else me, k)],
            dst_ref=piece.at[window(ward * rows + my_row, k)],
            send_sem=row_send.at[ward, target, k],
            recv_sem=row_recv.at[ward, my_row, k],
            device_id=(target, me),
            device_id_type=pl.DeviceIdType.MESH,
        )

    def row_arrive(step, ward, k):
        source = lax.rem(my_row + step, rows)
        pltpu.make_async_remote_copy(
            src_ref=piece.at[window(ward * rows + source, k)],
            dst_ref=piece.at[window(ward * rows + source, k)],
            send_sem=row_send.at[ward, source, k],
            recv_sem=row_recv.at[ward, source, k],
            device_id=(source, me),
            device_id_type=pl.DeviceIdType.MESH,
        ).wait_recv()

    def chip_rows(zz, xx):
        return pl.ds(pl.multiple_of(col_of(zz, xx, 0) * band, 2 * band), 2 * band)

    def lent_copy(zz, xx):
        return pltpu.make_async_remote_copy(
            src_ref=lent.at[chip_rows(zz, xx)],
            dst_ref=lent.at[chip_rows(zz, xx)],
            send_sem=lent_send.at[zz, xx],
            recv_sem=lent_recv.at[zz, xx],
            device_id=(my_row, ward_slot),
            device_id_type=pl.DeviceIdType.MESH,
        )

    end = (z == 0) | (z == line - 1)
    inner = jnp.logical_not(end)
    helper = (z == 1) | (z == line - 2)
    ward_z = jnp.where(z == 1, 0, jnp.where(end, jnp.where(z == 0, 1, line - 2), line - 1))
    ward_slot = col_of(ward_z, x, core)
    to_up = z < line - 2
    to_down = z > 1

    def goes_side(zz, k):
        far = (zz < z - 1) | (zz > z + 1)
        middle = (zz > 0) & (zz < line - 1) & (k >= SWAPPED)
        return (zz == z) | (inner & (far | middle))

    has_up = z < line - 1
    has_down = z > 0

    barrier = pltpu.get_barrier_semaphore()

    def greet(target):
        pl.semaphore_signal(barrier, inc=1, device_id=target, device_id_type=pl.DeviceIdType.MESH)

    greet(device(SIDE))
    greet(device(TWIN))
    for step in range(1, rows):
        greet((lax.rem(my_row + step, rows), me))

    @pl.when(has_up)
    def _():
        greet(device(UP))

    @pl.when(has_down)
    def _():
        greet(device(DOWN))

    root = jnp.sqrt(weight_ref[...])
    for k in range(PARTS):
        here = pl.ds(k * part, part)
        value = (root * pair_ref[here].astype(jnp.float32)).astype(jnp.bfloat16)
        held[window(me, k)] = value

        @pl.when(inner)
        def _():
            piece[window(my_row, k)] = value

    ends = (z == 0).astype(jnp.int32) + (z == line - 1).astype(jnp.int32)
    pl.semaphore_wait(barrier, 3 + rows - ends)
    beside = col_of(z, 1 - x, core)

    def act(begin, way, slot, k):
        if begin:
            copy(way, slot, k).start()
        else:
            copy(way, slot, k).wait_send()

    def tick(t, begin):
        d, k = t // PARTS, lax.rem(t, PARTS)
        low, high = z - d, z + d

        @pl.when(to_up & (low >= 0) & (inner | (d == 0)))
        def _():
            act(begin, UP, col_of(low, x, core), k)

        @pl.when(to_down & (high < line) & (inner | (d == 0)))
        def _():
            act(begin, DOWN, col_of(high, x, core), k)

        @pl.when(d == 0)
        def _():
            act(begin, SIDE, me, k)

            if begin:

                @pl.when(inner)
                def _():
                    copy(TWIN, me, k).start()
                    for step in range(1, rows):
                        row_copy(step, 0, k).start()

        if begin:

            @pl.when((t >= LAG) & (t < PARTS + LAG))
            def _():
                arrive(beside, t - LAG)

                @pl.when(inner)
                def _():
                    copy(TWIN, beside, t - LAG).start()

        swap = jnp.where(end, d == 1, (d == line - 2) & (k < SWAPPED))

        @pl.when(to_up & swap)
        def _():
            act(begin, UP, beside, k)

        @pl.when(to_down & swap)
        def _():
            act(begin, DOWN, beside, k)

        ahead = (t + SWAPPED) // PARTS
        part_ahead = lax.rem(t + SWAPPED, PARTS)

        def relay(zz):
            slot = col_of(zz, x, core)
            if begin:
                arrive(slot, part_ahead)
                copy(TWIN, slot, part_ahead).start()

                @pl.when(helper & (slot == ward_slot))
                def _():
                    piece[window(rows + my_row, part_ahead)] = held[window(slot, part_ahead)]
                    for step in range(1, rows):
                        row_copy(step, 1, part_ahead).start()

            @pl.when(goes_side(zz, part_ahead))
            def _():
                act(begin, SIDE, slot, part_ahead)

        @pl.when(inner & (ahead > 0) & (z - ahead >= 0))
        def _():
            relay(z - ahead)

        @pl.when(inner & (ahead > 0) & (z + ahead < line))
        def _():
            relay(z + ahead)

    ticks = PARTS * (line - 2) + SWAPPED

    def advance(t, _):
        @pl.when(t >= LAG)
        def _():
            tick(t - LAG, False)

        @pl.when(t < ticks)
        def _():
            tick(t, True)

        return 0

    lax.fori_loop(0, ticks, advance, 0)

    def row_wait(ward):
        def each(k, _):
            for step in range(1, rows):
                row_arrive(step, ward, k)
            return 0

        lax.fori_loop(0, PARTS, each, 0)

    @pl.when(inner)
    def _():
        row_wait(0)

    @pl.when(helper)
    def _():
        row_wait(1)

    def multiply(start, wide):
        return lax.dot_general(
            held[start], piece[: wide * band], (((1,), (1,)), ((), ())), preferred_element_type=jnp.float32
        )

    def product(zz, xx):
        def each(k, _):
            arrive(col_of(zz, xx, 1 - core), k)
            return 0

        lax.fori_loop(0, PARTS, each, 0)
        start = chip_rows(zz, xx)

        @pl.when(helper)
        def _():
            both = multiply(start, 2 * rows)
            lent[start] = both[:, rows * band :]
            lent_copy(zz, xx).start()
            out_ref[start] = both[:, : rows * band]

        if line > 4:

            @pl.when(jnp.logical_not(helper))
            def _():
                out_ref[start] = multiply(start, rows)

    def settle(t, _):
        d = t // 2
        zz = jnp.where(lax.rem(t, 2) == 0, z - d, z + d)

        @pl.when((zz >= 0) & (zz < line) & (t != 0))
        def _():
            def each(k, _):
                slot = col_of(zz, 1 - x, core)
                arrive(slot, k)
                copy(TWIN, slot, k).start()
                return 0

            product(zz, x)

            @pl.when(d > 0)
            def _():
                lax.fori_loop(0, PARTS, each, 0)

            product(zz, 1 - x)

        return 0

    @pl.when(inner)
    def _():
        lax.fori_loop(1, 2 * line, settle, 0)

    @pl.when(end)
    def _():
        def take(t, _):
            d = t // 2
            zz = jnp.where(z == 0, lax.rem(d + 1, line), lax.rem(2 * line - 2 - d, line))
            xx = lax.rem(x + t, 2)
            lent_copy(zz, xx).wait_recv()
            out_ref[chip_rows(zz, xx)] = lent[chip_rows(zz, xx)]
            return 0

        lax.fori_loop(0, 2 * line, take, 0)

    lax.fori_loop(ticks, ticks + LAG, advance, 0)

    @pl.when(inner)
    def _():
        def drain(zz, _):
            def each(k, _):
                for xx in range(2):
                    copy(TWIN, col_of(zz, xx, core), k).wait_send()
                return 0

            lax.fori_loop(0, PARTS, each, 0)

            @pl.when(helper)
            def _():
                for xx in range(2):
                    lent_copy(zz, xx).wait_send()

            return 0

        lax.fori_loop(0, line, drain, 0)

    def last(k, _):
        for step in range(1, rows):

            @pl.when(inner)
            def _():
                row_copy(step, 0, k).wait_send()

            @pl.when(helper)
            def _():
                row_copy(step, 1, k).wait_send()

        return 0

    lax.fori_loop(0, PARTS, last, 0)


def on_device(rows, cols, pair_density, coulomb):
    band, comps = pair_density.shape
    weight = coulomb[None, :]
    vmem = pl.BlockSpec(memory_space=pltpu.VMEM)
    kernel = pl.pallas_call(
        functools.partial(body, rows, cols),
        out_shape=jax.ShapeDtypeStruct((cols * band, rows * band), jnp.float32),
        in_specs=[vmem, vmem],
        out_specs=vmem,
        scratch_shapes=[
            pltpu.VMEM((cols * band, comps), jnp.bfloat16),
            pltpu.VMEM((2 * rows * band, comps), jnp.bfloat16),
            pltpu.VMEM((cols * band, rows * band), jnp.float32),
            pltpu.SemaphoreType.DMA((4, cols, PARTS)),
            pltpu.SemaphoreType.DMA((cols, PARTS)),
            pltpu.SemaphoreType.DMA((2, rows, PARTS)),
            pltpu.SemaphoreType.DMA((2, rows, PARTS)),
            pltpu.SemaphoreType.DMA((cols // 4, 2)),
            pltpu.SemaphoreType.DMA((cols // 4, 2)),
        ],
        compiler_params=pltpu.CompilerParams(
            collective_id=0, has_side_effects=True, vmem_limit_bytes=48 * 1024 * 1024
        ),
        cost_estimate=pl.CostEstimate(
            flops=2 * cols * rows * band * band * comps,
            bytes_accessed=2 * band * comps + 4 * cols * rows * band * band,
            transcendentals=0,
        ),
    )(pair_density, weight)
    return kernel.reshape(cols * band, 1, rows * band)


def solution(mesh):
    rows, cols = mesh.shape["row"], mesh.shape["col"]
    in_specs = (P(("row", "col"), None), P())
    out_specs = P("row", "col", None)
    return jax.shard_map(
        functools.partial(on_device, rows, cols),
        mesh=mesh,
        in_specs=in_specs,
        out_specs=out_specs,
        check_vma=False,
    )
```

```python
import functools

import jax
import jax.numpy as jnp
from jax import lax
from jax.experimental import pallas as pl
from jax.experimental.pallas import tpu as pltpu
from jax.sharding import PartitionSpec as P

UP, DOWN, SIDE, TWIN = range(4)
PARTS = 2
SWAPPED = 1
LAG = 2


def body(rows, cols, pair_ref, weight_ref, out_ref, held, piece, lent, *sems):
    send_sem, recv_sem, row_send, row_recv, lent_send, lent_recv = sems
    band = pair_ref.shape[0]
    part = band // PARTS
    line = cols // 4
    my_row = lax.axis_index("row")
    me = lax.axis_index("col")
    core = lax.rem(me, 2)
    x = lax.rem(me // 2, 2)
    z = me // 4

    def col_of(zz, xx, cc):
        return (zz * 2 + xx) * 2 + cc

    def device(way):
        if way == UP:
            target = col_of(z + 1, x, core)
        elif way == DOWN:
            target = col_of(z - 1, x, core)
        elif way == SIDE:
            target = col_of(z, 1 - x, core)
        else:
            target = col_of(z, x, 1 - core)
        return (my_row, target)

    def window(slot, k):
        return pl.ds(pl.multiple_of(slot * band + k * part, part), part)

    def copy(way, slot, k):
        return pltpu.make_async_remote_copy(
            src_ref=held.at[window(slot, k)],
            dst_ref=held.at[window(slot, k)],
            send_sem=send_sem.at[way, slot, k],
            recv_sem=recv_sem.at[slot, k],
            device_id=device(way),
            device_id_type=pl.DeviceIdType.MESH,
        )

    def arrive(slot, k):
        copy(SIDE, slot, k).wait_recv()

    def row_copy(step, ward, k):
        target = lax.rem(my_row + step, rows)
        return pltpu.make_async_remote_copy(
            src_ref=held.at[window(ward_slot if ward else me, k)],
            dst_ref=piece.at[window(ward * rows + my_row, k)],
            send_sem=row_send.at[ward, target, k],
            recv_sem=row_recv.at[ward, my_row, k],
            device_id=(target, me),
            device_id_type=pl.DeviceIdType.MESH,
        )

    def row_arrive(step, ward, k):
        source = lax.rem(my_row + step, rows)
        pltpu.make_async_remote_copy(
            src_ref=piece.at[window(ward * rows + source, k)],
            dst_ref=piece.at[window(ward * rows + source, k)],
            send_sem=row_send.at[ward, source, k],
            recv_sem=row_recv.at[ward, source, k],
            device_id=(source, me),
            device_id_type=pl.DeviceIdType.MESH,
        ).wait_recv()

    def chip_rows(zz, xx):
        return pl.ds(pl.multiple_of(col_of(zz, xx, 0) * band, 2 * band), 2 * band)

    def lent_copy(zz, xx):
        return pltpu.make_async_remote_copy(
            src_ref=lent.at[chip_rows(zz, xx)],
            dst_ref=lent.at[chip_rows(zz, xx)],
            send_sem=lent_send.at[zz, xx],
            recv_sem=lent_recv.at[zz, xx],
            device_id=(my_row, ward_slot),
            device_id_type=pl.DeviceIdType.MESH,
        )

    end = (z == 0) | (z == line - 1)
    inner = jnp.logical_not(end)
    helper = (z == 1) | (z == line - 2)
    ward_z = jnp.where(z == 1, 0, jnp.where(end, jnp.where(z == 0, 1, line - 2), line - 1))
    ward_slot = col_of(ward_z, x, core)
    to_up = z < line - 2
    to_down = z > 1

    def goes_side(zz, k):
        far = (zz < z - 1) | (zz > z + 1)
        middle = (zz > 0) & (zz < line - 1) & (k >= SWAPPED)
        return (zz == z) | (inner & (far | middle))

    has_up = z < line - 1
    has_down = z > 0

    barrier = pltpu.get_barrier_semaphore()

    def greet(target):
        pl.semaphore_signal(barrier, inc=1, device_id=target, device_id_type=pl.DeviceIdType.MESH)

    greet(device(SIDE))
    greet(device(TWIN))
    for step in range(1, rows):
        greet((lax.rem(my_row + step, rows), me))

    @pl.when(has_up)
    def _():
        greet(device(UP))

    @pl.when(has_down)
    def _():
        greet(device(DOWN))

    root = jnp.sqrt(weight_ref[...])
    for k in range(PARTS):
        here = pl.ds(k * part, part)
        value = (root * pair_ref[here].astype(jnp.float32)).astype(jnp.bfloat16)
        held[window(me, k)] = value

        @pl.when(inner)
        def _():
            piece[window(my_row, k)] = value

    ends = (z == 0).astype(jnp.int32) + (z == line - 1).astype(jnp.int32)
    pl.semaphore_wait(barrier, 3 + rows - ends)
    beside = col_of(z, 1 - x, core)

    def act(begin, way, slot, k):
        if begin:
            copy(way, slot, k).start()
        else:
            copy(way, slot, k).wait_send()

    def tick(t, begin):
        d, k = t // PARTS, lax.rem(t, PARTS)
        low, high = z - d, z + d

        @pl.when(to_up & (low >= 0) & (inner | (d == 0)))
        def _():
            act(begin, UP, col_of(low, x, core), k)

        @pl.when(to_down & (high < line) & (inner | (d == 0)))
        def _():
            act(begin, DOWN, col_of(high, x, core), k)

        @pl.when(d == 0)
        def _():
            act(begin, SIDE, me, k)

            if begin:

                @pl.when(inner)
                def _():
                    copy(TWIN, me, k).start()
                    for step in range(1, rows):
                        row_copy(step, 0, k).start()

        if begin:

            @pl.when((t >= LAG) & (t < PARTS + LAG))
            def _():
                arrive(beside, t - LAG)

                @pl.when(inner)
                def _():
                    copy(TWIN, beside, t - LAG).start()

        swap = jnp.where(end, d == 1, (d == line - 2) & (k < SWAPPED))

        @pl.when(to_up & swap)
        def _():
            act(begin, UP, beside, k)

        @pl.when(to_down & swap)
        def _():
            act(begin, DOWN, beside, k)

        ahead = (t + SWAPPED) // PARTS
        part_ahead = lax.rem(t + SWAPPED, PARTS)

        def relay(zz):
            slot = col_of(zz, x, core)
            if begin:
                arrive(slot, part_ahead)
                copy(TWIN, slot, part_ahead).start()

                @pl.when(helper & (slot == ward_slot))
                def _():
                    piece[window(rows + my_row, part_ahead)] = held[window(slot, part_ahead)]
                    for step in range(1, rows):
                        row_copy(step, 1, part_ahead).start()

            @pl.when(goes_side(zz, part_ahead))
            def _():
                act(begin, SIDE, slot, part_ahead)

        @pl.when(inner & (ahead > 0) & (z - ahead >= 0))
        def _():
            relay(z - ahead)

        @pl.when(inner & (ahead > 0) & (z + ahead < line))
        def _():
            relay(z + ahead)

    ticks = PARTS * (line - 2) + SWAPPED

    def advance(t, _):
        @pl.when(t >= LAG)
        def _():
            tick(t - LAG, False)

        @pl.when(t < ticks)
        def _():
            tick(t, True)

        return 0

    lax.fori_loop(0, ticks, advance, 0)

    def row_wait(ward):
        def each(k, _):
            for step in range(1, rows):
                row_arrive(step, ward, k)
            return 0

        lax.fori_loop(0, PARTS, each, 0)

    @pl.when(inner)
    def _():
        row_wait(0)

    @pl.when(helper)
    def _():
        row_wait(1)

    def multiply(start, wide):
        return lax.dot_general(
            held[start], piece[: wide * band], (((1,), (1,)), ((), ())), preferred_element_type=jnp.float32
        )

    def product(zz, xx):
        def each(k, _):
            arrive(col_of(zz, xx, 1 - core), k)
            return 0

        lax.fori_loop(0, PARTS, each, 0)
        start = chip_rows(zz, xx)

        @pl.when(helper)
        def _():
            both = multiply(start, 2 * rows)
            lent[start] = both[:, rows * band :]
            lent_copy(zz, xx).start()
            out_ref[start] = both[:, : rows * band]

        if line > 4:

            @pl.when(jnp.logical_not(helper))
            def _():
                out_ref[start] = multiply(start, rows)

    def settle(t, _):
        d = t // 2
        zz = jnp.where(lax.rem(t, 2) == 0, z - d, z + d)

        @pl.when((zz >= 0) & (zz < line) & (t != 0))
        def _():
            def each(k, _):
                slot = col_of(zz, 1 - x, core)
                arrive(slot, k)
                copy(TWIN, slot, k).start()
                return 0

            product(zz, x)

            @pl.when(d > 0)
            def _():
                lax.fori_loop(0, PARTS, each, 0)

            product(zz, 1 - x)

        return 0

    @pl.when(inner)
    def _():
        lax.fori_loop(1, 2 * line, settle, 0)

    @pl.when(end)
    def _():
        def take(t, _):
            d = t // 2
            zz = jnp.where(z == 0, lax.rem(d + 1, line), lax.rem(2 * line - 2 - d, line))
            xx = lax.rem(x + t, 2)
            lent_copy(zz, xx).wait_recv()
            out_ref[chip_rows(zz, xx)] = lent[chip_rows(zz, xx)]
            return 0

        lax.fori_loop(0, 2 * line, take, 0)

    lax.fori_loop(ticks, ticks + LAG, advance, 0)

    @pl.when(inner)
    def _():
        def drain(zz, _):
            def each(k, _):
                for xx in range(2):
                    copy(TWIN, col_of(zz, xx, core), k).wait_send()
                return 0

            lax.fori_loop(0, PARTS, each, 0)

            @pl.when(helper)
            def _():
                for xx in range(2):
                    lent_copy(zz, xx).wait_send()

            return 0

        lax.fori_loop(0, line, drain, 0)

    def last(k, _):
        for step in range(1, rows):

            @pl.when(inner)
            def _():
                row_copy(step, 0, k).wait_send()

            @pl.when(helper)
            def _():
                row_copy(step, 1, k).wait_send()

        return 0

    lax.fori_loop(0, PARTS, last, 0)


def on_device(rows, cols, pair_density, coulomb):
    band, comps = pair_density.shape
    weight = coulomb[None, :]
    vmem = pl.BlockSpec(memory_space=pltpu.VMEM)
    kernel = pl.pallas_call(
        functools.partial(body, rows, cols),
        out_shape=jax.ShapeDtypeStruct((cols * band, rows * band), jnp.float32),
        in_specs=[vmem, vmem],
        out_specs=vmem,
        scratch_shapes=[
            pltpu.VMEM((cols * band, comps), jnp.bfloat16),
            pltpu.VMEM((2 * rows * band, comps), jnp.bfloat16),
            pltpu.VMEM((cols * band, rows * band), jnp.float32),
            pltpu.SemaphoreType.DMA((4, cols, PARTS)),
            pltpu.SemaphoreType.DMA((cols, PARTS)),
            pltpu.SemaphoreType.DMA((2, rows, PARTS)),
            pltpu.SemaphoreType.DMA((2, rows, PARTS)),
            pltpu.SemaphoreType.DMA((cols // 4, 2)),
            pltpu.SemaphoreType.DMA((cols // 4, 2)),
        ],
        compiler_params=pltpu.CompilerParams(
            collective_id=0, has_side_effects=True, vmem_limit_bytes=48 * 1024 * 1024
        ),
        cost_estimate=pl.CostEstimate(
            flops=2 * cols * rows * band * band * comps,
            bytes_accessed=2 * band * comps + 4 * cols * rows * band * band,
            transcendentals=0,
        ),
    )(pair_density, weight)
    return kernel.reshape(cols * band, 1, rows * band)


def solution(mesh):
    rows, cols = mesh.shape["row"], mesh.shape["col"]
    in_specs = (P(("row", "col"), None), P())
    out_specs = P("row", "col", None)
    return jax.shard_map(
        functools.partial(on_device, rows, cols),
        mesh=mesh,
        in_specs=in_specs,
        out_specs=out_specs,
        check_vma=False,
    )
```

```python
import functools

import jax
import jax.numpy as jnp
from jax import lax
from jax.experimental import pallas as pl
from jax.experimental.pallas import tpu as pltpu
from jax.sharding import PartitionSpec as P

UP, DOWN, SIDE, TWIN = range(4)
PARTS = 2
SWAPPED = 1
LAG = 2


def body(rows, cols, pair_ref, weight_ref, out_ref, held, piece, lent, *sems):
    send_sem, recv_sem, row_send, row_recv, lent_send, lent_recv = sems
    band = pair_ref.shape[0]
    part = band // PARTS
    line = cols // 4
    my_row = lax.axis_index("row")
    me = lax.axis_index("col")
    core = lax.rem(me, 2)
    x = lax.rem(me // 2, 2)
    z = me // 4

    def col_of(zz, xx, cc):
        return (zz * 2 + xx) * 2 + cc

    def device(way):
        if way == UP:
            target = col_of(z + 1, x, core)
        elif way == DOWN:
            target = col_of(z - 1, x, core)
        elif way == SIDE:
            target = col_of(z, 1 - x, core)
        else:
            target = col_of(z, x, 1 - core)
        return (my_row, target)

    def window(slot, k):
        return pl.ds(pl.multiple_of(slot * band + k * part, part), part)

    def copy(way, slot, k):
        return pltpu.make_async_remote_copy(
            src_ref=held.at[window(slot, k)],
            dst_ref=held.at[window(slot, k)],
            send_sem=send_sem.at[way, slot, k],
            recv_sem=recv_sem.at[slot, k],
            device_id=device(way),
            device_id_type=pl.DeviceIdType.MESH,
        )

    def arrive(slot, k):
        copy(SIDE, slot, k).wait_recv()

    def row_copy(step, ward, k):
        target = lax.rem(my_row + step, rows)
        return pltpu.make_async_remote_copy(
            src_ref=held.at[window(ward_slot if ward else me, k)],
            dst_ref=piece.at[window(ward * rows + my_row, k)],
            send_sem=row_send.at[ward, target, k],
            recv_sem=row_recv.at[ward, my_row, k],
            device_id=(target, me),
            device_id_type=pl.DeviceIdType.MESH,
        )

    def row_arrive(step, ward, k):
        source = lax.rem(my_row + step, rows)
        pltpu.make_async_remote_copy(
            src_ref=piece.at[window(ward * rows + source, k)],
            dst_ref=piece.at[window(ward * rows + source, k)],
            send_sem=row_send.at[ward, source, k],
            recv_sem=row_recv.at[ward, source, k],
            device_id=(source, me),
            device_id_type=pl.DeviceIdType.MESH,
        ).wait_recv()

    def chip_rows(zz, xx):
        return pl.ds(pl.multiple_of(col_of(zz, xx, 0) * band, 2 * band), 2 * band)

    def lent_copy(zz, xx):
        return pltpu.make_async_remote_copy(
            src_ref=lent.at[chip_rows(zz, xx)],
            dst_ref=lent.at[chip_rows(zz, xx)],
            send_sem=lent_send.at[zz, xx],
            recv_sem=lent_recv.at[zz, xx],
            device_id=(my_row, ward_slot),
            device_id_type=pl.DeviceIdType.MESH,
        )

    end = (z == 0) | (z == line - 1)
    inner = jnp.logical_not(end)
    helper = (z == 1) | (z == line - 2)
    ward_z = jnp.where(z == 1, 0, jnp.where(end, jnp.where(z == 0, 1, line - 2), line - 1))
    ward_slot = col_of(ward_z, x, core)
    to_up = z < line - 2
    to_down = z > 1

    def goes_side(zz, k):
        far = (zz < z - 1) | (zz > z + 1)
        middle = (zz > 0) & (zz < line - 1) & (k >= SWAPPED)
        return (zz == z) | (inner & (far | middle))

    has_up = z < line - 1
    has_down = z > 0

    barrier = pltpu.get_barrier_semaphore()

    def greet(target):
        pl.semaphore_signal(barrier, inc=1, device_id=target, device_id_type=pl.DeviceIdType.MESH)

    greet(device(SIDE))
    greet(device(TWIN))
    for step in range(1, rows):
        greet((lax.rem(my_row + step, rows), me))

    @pl.when(has_up)
    def _():
        greet(device(UP))

    @pl.when(has_down)
    def _():
        greet(device(DOWN))

    root = jnp.sqrt(weight_ref[...])

    def scale(k):
        here = pl.ds(k * part, part)
        value = (root * pair_ref[here].astype(jnp.float32)).astype(jnp.bfloat16)
        held[window(me, k)] = value

        @pl.when(inner)
        def _():
            piece[window(my_row, k)] = value

    scale(0)
    ends = (z == 0).astype(jnp.int32) + (z == line - 1).astype(jnp.int32)
    pl.semaphore_wait(barrier, 3 + rows - ends)
    beside = col_of(z, 1 - x, core)

    def act(begin, way, slot, k):
        if begin:
            copy(way, slot, k).start()
        else:
            copy(way, slot, k).wait_send()

    def tick(t, begin):
        d, k = t // PARTS, lax.rem(t, PARTS)
        low, high = z - d, z + d

        @pl.when(to_up & (low >= 0) & (inner | (d == 0)))
        def _():
            act(begin, UP, col_of(low, x, core), k)

        @pl.when(to_down & (high < line) & (inner | (d == 0)))
        def _():
            act(begin, DOWN, col_of(high, x, core), k)

        @pl.when(d == 0)
        def _():
            act(begin, SIDE, me, k)

            if begin:

                @pl.when(inner)
                def _():
                    copy(TWIN, me, k).start()
                    for step in range(1, rows):
                        row_copy(step, 0, k).start()

        if begin:

            @pl.when((t >= LAG) & (t < PARTS + LAG))
            def _():
                arrive(beside, t - LAG)

                @pl.when(inner)
                def _():
                    copy(TWIN, beside, t - LAG).start()

        swap = jnp.where(end, d == 1, (d == line - 2) & (k < SWAPPED))

        @pl.when(to_up & swap)
        def _():
            act(begin, UP, beside, k)

        @pl.when(to_down & swap)
        def _():
            act(begin, DOWN, beside, k)

        ahead = (t + SWAPPED) // PARTS
        part_ahead = lax.rem(t + SWAPPED, PARTS)

        def relay(zz):
            slot = col_of(zz, x, core)
            if begin:
                arrive(slot, part_ahead)
                copy(TWIN, slot, part_ahead).start()

                @pl.when(helper & (slot == ward_slot))
                def _():
                    piece[window(rows + my_row, part_ahead)] = held[window(slot, part_ahead)]
                    for step in range(1, rows):
                        row_copy(step, 1, part_ahead).start()

            @pl.when(goes_side(zz, part_ahead))
            def _():
                act(begin, SIDE, slot, part_ahead)

        @pl.when(inner & (ahead > 0) & (z - ahead >= 0))
        def _():
            relay(z - ahead)

        @pl.when(inner & (ahead > 0) & (z + ahead < line))
        def _():
            relay(z + ahead)

    ticks = PARTS * (line - 2) + SWAPPED

    def advance(t, _):
        @pl.when(t >= LAG)
        def _():
            tick(t - LAG, False)

        @pl.when(t < ticks)
        def _():
            tick(t, True)

        return 0

    advance(jnp.int32(0), 0)
    for k in range(1, PARTS):
        scale(k)
    lax.fori_loop(1, ticks, advance, 0)

    def row_wait(ward):
        def each(k, _):
            for step in range(1, rows):
                row_arrive(step, ward, k)
            return 0

        lax.fori_loop(0, PARTS, each, 0)

    @pl.when(inner)
    def _():
        row_wait(0)

    @pl.when(helper)
    def _():
        row_wait(1)

    def multiply(start, wide):
        return lax.dot_general(
            held[start], piece[: wide * band], (((1,), (1,)), ((), ())), preferred_element_type=jnp.float32
        )

    def product(zz, xx):
        def each(k, _):
            arrive(col_of(zz, xx, 1 - core), k)
            return 0

        lax.fori_loop(0, PARTS, each, 0)
        start = chip_rows(zz, xx)

        @pl.when(helper)
        def _():
            both = multiply(start, 2 * rows)
            lent[start] = both[:, rows * band :]
            lent_copy(zz, xx).start()
            out_ref[start] = both[:, : rows * band]

        if line > 4:

            @pl.when(jnp.logical_not(helper))
            def _():
                out_ref[start] = multiply(start, rows)

    def settle(t, _):
        d = t // 2
        zz = jnp.where(lax.rem(t, 2) == 0, z - d, z + d)

        @pl.when((zz >= 0) & (zz < line) & (t != 0))
        def _():
            def each(k, _):
                slot = col_of(zz, 1 - x, core)
                arrive(slot, k)
                copy(TWIN, slot, k).start()
                return 0

            product(zz, x)

            @pl.when(d > 0)
            def _():
                lax.fori_loop(0, PARTS, each, 0)

            product(zz, 1 - x)

        return 0

    @pl.when(inner)
    def _():
        lax.fori_loop(1, 2 * line, settle, 0)

    @pl.when(end)
    def _():
        def take(t, _):
            d = t // 2
            zz = jnp.where(z == 0, lax.rem(d + 1, line), lax.rem(2 * line - 2 - d, line))
            xx = lax.rem(x + t, 2)
            lent_copy(zz, xx).wait_recv()
            out_ref[chip_rows(zz, xx)] = lent[chip_rows(zz, xx)]
            return 0

        lax.fori_loop(0, 2 * line, take, 0)

    lax.fori_loop(ticks, ticks + LAG, advance, 0)

    @pl.when(inner)
    def _():
        def drain(zz, _):
            def each(k, _):
                for xx in range(2):
                    copy(TWIN, col_of(zz, xx, core), k).wait_send()
                return 0

            lax.fori_loop(0, PARTS, each, 0)

            @pl.when(helper)
            def _():
                for xx in range(2):
                    lent_copy(zz, xx).wait_send()

            return 0

        lax.fori_loop(0, line, drain, 0)

    def last(k, _):
        for step in range(1, rows):

            @pl.when(inner)
            def _():
                row_copy(step, 0, k).wait_send()

            @pl.when(helper)
            def _():
                row_copy(step, 1, k).wait_send()

        return 0

    lax.fori_loop(0, PARTS, last, 0)


def on_device(rows, cols, pair_density, coulomb):
    band, comps = pair_density.shape
    weight = coulomb[None, :]
    vmem = pl.BlockSpec(memory_space=pltpu.VMEM)
    kernel = pl.pallas_call(
        functools.partial(body, rows, cols),
        out_shape=jax.ShapeDtypeStruct((cols * band, rows * band), jnp.float32),
        in_specs=[vmem, vmem],
        out_specs=vmem,
        scratch_shapes=[
            pltpu.VMEM((cols * band, comps), jnp.bfloat16),
            pltpu.VMEM((2 * rows * band, comps), jnp.bfloat16),
            pltpu.VMEM((cols * band, rows * band), jnp.float32),
            pltpu.SemaphoreType.DMA((4, cols, PARTS)),
            pltpu.SemaphoreType.DMA((cols, PARTS)),
            pltpu.SemaphoreType.DMA((2, rows, PARTS)),
            pltpu.SemaphoreType.DMA((2, rows, PARTS)),
            pltpu.SemaphoreType.DMA((cols // 4, 2)),
            pltpu.SemaphoreType.DMA((cols // 4, 2)),
        ],
        compiler_params=pltpu.CompilerParams(
            collective_id=0, has_side_effects=True, vmem_limit_bytes=48 * 1024 * 1024
        ),
        cost_estimate=pl.CostEstimate(
            flops=2 * cols * rows * band * band * comps,
            bytes_accessed=2 * band * comps + 4 * cols * rows * band * band,
            transcendentals=0,
        ),
    )(pair_density, weight)
    return kernel.reshape(cols * band, 1, rows * band)


def solution(mesh):
    rows, cols = mesh.shape["row"], mesh.shape["col"]
    in_specs = (P(("row", "col"), None), P())
    out_specs = P("row", "col", None)
    return jax.shard_map(
        functools.partial(on_device, rows, cols),
        mesh=mesh,
        in_specs=in_specs,
        out_specs=out_specs,
        check_vma=False,
    )
```
